256 devices in a mesh: dp: 8 (over y, core), layer: 8 (over z), tensor: 4 (over x).
Axes of the slice: x: 4, y: 4, z: 8, core: 2. Of those that a mesh axis runs over, the one named last changes fastest.
Arguments:
- train_acts: bfloat16 [8, 1024, 8192], P('layer', ('dp', 'tensor')), may hold values from -6 to 6
- train_grads: bfloat16 [8, 1024, 14336], P('layer', ('dp', 'tensor')), may hold values from -6 to 6
- query_acts: bfloat16 [8, 512, 8192], P('layer', ('dp', 'tensor')), may hold values from -6 to 6
- query_grads: bfloat16 [8, 512, 14336], P('layer', ('dp', 'tensor')), may hold values from -6 to 6
- in_basis: bfloat16 [8, 8192, 8192], P('layer', None, ('dp', 'tensor')), may hold values from -0.0625 to 0.0625
- out_basis: bfloat16 [8, 14336, 128], P('layer', 'tensor'), may hold values from -0.046875 to 0.046875
- eig_values: float32 [8, 128, 8192], P('layer', None, ('dp', 'tensor')), may hold values from 0.0003 to 30
- vote_of_query: int32 [64], replicated, may hold values from 0 to 7
Outputs:
- scores: float32 [8, 8], replicated
The draws below stay inside these ranges and needn't reach their ends.
All inputs are finite; a program needn't handle non-finite values.
Results may differ from the reference program's by a relative error of at most 0.0056.
Values may be sent and summed in bfloat16 or wider, within the bound.
No kernel may reach another device: no remote copies, remote signals or barrier semaphores. Data moves between devices by JAX's collectives and lax.ppermute only.
A program may use at most 128 MiB of HBM per device.

```python
import math
import jax
import jax.numpy as jnp
from jax import lax

D = 8192
FFW = 14336
KS = 128
Q = 64
QT = 8
SEQ_TOK = 128
VOTES = 8
LAYERS = 8
TOKENS = 1024
SEQS = 8
QTOK = 512


def draw_eig_values(key, part):
    key = jax.random.fold_in(key, 7)
    first_key, second_key = jax.random.split(key)
    ramp = jnp.arange(D, dtype=jnp.float32) / (D - 1)
    base = jnp.exp(jax.random.uniform(first_key, (LAYERS, KS, D), jnp.float32, math.log(0.001), 0.0))
    slope = 2.0
    row_scale = jnp.exp(jax.random.uniform(second_key, (LAYERS, KS, 1), jnp.float32, 0.0, math.log(10.0)))
    return base * row_scale * (1.0 + slope * ramp)


def touch_ends(result, key, low, high):
    longest = result.shape.index(max(result.shape))
    spots = []
    for shift in (0, 1):
        where = [jax.random.randint(jax.random.fold_in(key, axis), (), 0, length) for axis, length in enumerate(result.shape)]
        where[longest] = (where[longest] + shift) % result.shape[longest]
        spots.append(tuple(where))
    return result.at[spots[0]].set(low).at[spots[1]].set(high)


def steps_of(rng, dims, cuts, smallest, high):
    factor_of = 1.0
    for position, shards_of in cuts:
        heights = jax.random.uniform(jax.random.fold_in(jax.random.fold_in(rng, 6), position), (shards_of,), jnp.float32, smallest / len(cuts), high / len(cuts))
        factor_of = factor_of * jnp.repeat(jnp.exp(heights), dims[position] // shards_of).reshape((-1,) + (1,) * (len(dims) - 1 - position))
    return factor_of


def normal_values(own_key, shape, width, bound, cuts=(), kind=jnp.bfloat16):
    gain = steps_of(own_key, shape, cuts, -0.22, 0.18) if cuts else 1.0
    entries = jax.random.normal(own_key, shape, jnp.float32) * width * gain
    return jnp.minimum(jnp.maximum(entries, -bound), bound).astype(kind)


def setup_inputs(seed: int = 0) -> dict:
    seeds = jax.random.split(jax.random.key(seed), 9)
    train_acts = normal_values(seeds[0], (LAYERS, TOKENS, D), 1.0, 6.0, ((0, 8), (1, 32)))
    train_grads = normal_values(seeds[1], (LAYERS, TOKENS, FFW), 1.0, 6.0, ((0, 8), (1, 32)))
    query_acts = normal_values(seeds[2], (LAYERS, QTOK, D), 1.0, 6.0, ((0, 8), (1, 32)))
    query_grads = normal_values(seeds[3], (LAYERS, QTOK, FFW), 1.0, 6.0, ((0, 8), (1, 32)))
    in_basis = normal_values(seeds[4], (LAYERS, D, D), D ** -0.5, 0.0625, ((0, 8), (2, 32)))
    out_basis = normal_values(seeds[5], (LAYERS, FFW, KS), FFW ** -0.5, 0.046875, ((0, 8), (1, 4)))
    eig_values = draw_eig_values(jax.random.fold_in(seeds[8], 71), 0)
    vote_of_query = touch_ends(jax.random.randint(seeds[7], (Q,), 0, VOTES), jax.random.fold_in(seeds[7], 1), 0, VOTES - 1).astype(jnp.int32)
    return {"train_acts": train_acts, "train_grads": train_grads, "query_acts": query_acts, "query_grads": query_grads, "in_basis": in_basis, "out_basis": out_basis, "eig_values": eig_values, "vote_of_query": vote_of_query}


def reference(train_acts, train_grads, query_acts, query_grads, in_basis, out_basis, eig_values, vote_of_query):
    score_scale = 1.0 / math.sqrt(KS * D * LAYERS * Q)
    totals = jnp.zeros((TOKENS, Q), jnp.float32)
    for layer_index in range(LAYERS):
        train_out = jnp.dot(train_grads[layer_index], out_basis[layer_index], preferred_element_type=jnp.float32).astype(jnp.bfloat16)
        query_out = jnp.dot(query_grads[layer_index], out_basis[layer_index], preferred_element_type=jnp.float32).astype(jnp.bfloat16)
        train_in = jnp.dot(train_acts[layer_index], in_basis[layer_index], preferred_element_type=jnp.float32).astype(jnp.bfloat16)
        query_in = jnp.dot(query_acts[layer_index], in_basis[layer_index], preferred_element_type=jnp.float32).astype(jnp.bfloat16)
        damping = 0.1 * jnp.mean(eig_values[layer_index])
        query_rot = jnp.einsum('qts,qtd->qsd', query_out.reshape(Q, QT, KS).astype(jnp.float32), query_in.reshape(Q, QT, D).astype(jnp.float32))
        precond = (query_rot / (eig_values[layer_index] + damping)).astype(jnp.bfloat16).reshape(Q * KS, D)
        mixed_all = jnp.dot(train_in, precond.T, preferred_element_type=jnp.float32).reshape(TOKENS, Q, KS)
        totals = totals + jnp.einsum('tqs,ts->tq', mixed_all, train_out.astype(jnp.float32))
    totals = totals * score_scale
    per_seq = totals.reshape(SEQS, SEQ_TOK, Q).sum(axis=1)
    onehot = (vote_of_query[None, :] == jnp.arange(VOTES)[:, None]).astype(jnp.float32)
    return jnp.dot(onehot, per_seq.T, precision=lax.Precision.HIGHEST)
```

```python
import math

import jax
import jax.numpy as jnp
import numpy as np
from jax import lax
from jax.experimental import pallas as pl
from jax.experimental.pallas import tpu as pltpu
from jax.sharding import Mesh
from jax.sharding import PartitionSpec as P

QT = 8
SEQ_TOK = 128
VOTES = 8
RING = 4


def shift(a, axis, step):
    n = lax.axis_size(axis)
    return lax.ppermute(a, axis, [(i, (i + step) % n) for i in range(n)])


class Rows:
    def __init__(self, parts):
        self.parts = parts

    def cut(self, low, high):
        parts, at = [], 0
        for dx, dy, first, count in self.parts:
            a, b = max(low, at), min(high, at + count)
            if a < b:
                parts.append((dx, dy, first + a - at, b - a))
            at += count
        return Rows(parts)


def cut(a, low, high):
    return a.cut(low, high) if isinstance(a, Rows) else lax.slice_in_dim(a, low, high, axis=0)


def cat(parts):
    if isinstance(parts[0], Rows):
        return Rows([entry for part in parts for entry in part.parts])
    return jnp.concatenate(parts, axis=0)


def send(a, axis, step):
    if isinstance(a, Rows):
        mx, my = (step, 0) if axis == "tensor" else (0, step)
        return Rows([((dx - mx) % RING, (dy - my) % RING, f, n) for dx, dy, f, n in a.parts])
    return shift(a, axis, step)


def spread_1(o):
    return [send(o, "tensor", 1), send(o, "tensor", -1), send(o, "y", 1), send(o, "y", -1)]


def spread_2(r1, rows, half):
    west, east, south, north = r1
    q1, q2 = half // 2, (rows - half) // 2
    first = lambda a: [cut(a, 0, q1), cut(a, half, half + q2)]
    second = lambda a: [cut(a, q1, half), cut(a, half + q2, rows)]
    tops = lambda a: cut(a, 0, half)
    tails = lambda a: cut(a, half, rows)
    return [
        send(cat(first(west) + [tails(north), tails(south)]), "tensor", 1),
        send(cat(second(east) + [tails(north), tails(south)]), "tensor", -1),
        send(cat(first(south) + [tops(east), tops(west)]), "y", 1),
        send(cat(second(north) + [tops(east), tops(west)]), "y", -1),
    ]


def spread_3(r2, rows, half):
    a, b, c, d = r2
    q1, q2 = half // 2, (rows - half) // 2
    m = q1 + q2
    far_y = [cut(c, q1, m), cut(d, q1, m)]
    far_x = [cut(a, 0, q1), cut(b, 0, q1)]
    return [
        send(cat(far_y + [cut(a, m, m + q2), cut(a, m + 2 * q2, m + 3 * q2)]), "tensor", 1),
        send(cat(far_y + [cut(b, m + q2, m + 2 * q2), cut(b, m + 3 * q2, m + 4 * q2)]), "tensor", -1),
        send(cat(far_x + [cut(c, m, m + q1), cut(c, m + 2 * q1, m + 3 * q1)]), "y", 1),
        send(cat(far_x + [cut(d, m + q1, m + 2 * q1), cut(d, m + 3 * q1, m + 4 * q1)]), "y", -1),
    ]


def spread_4(r3, rows, half):
    e, f, g, h = r3
    q1, q2 = half // 2, (rows - half) // 2
    return [
        send(cut(e, 0, q2), "tensor", 1),
        send(cut(f, q2, 2 * q2), "tensor", -1),
        send(cut(g, 0, q1), "y", 1),
        send(cut(h, q1, 2 * q1), "y", -1),
    ]


def order_of(rows, half):
    own = Rows([(0, 0, 0, rows)])
    r1 = spread_1(own)
    r2 = spread_2(r1, rows, half)
    r3 = spread_3(r2, rows, half)
    r4 = spread_4(r3, rows, half)
    rounds = []
    for messages in ([own] + r1, r2, r3, r4):
        rounds.append(
            np.array([(dx, dy, f + i) for m in messages for dx, dy, f, n in m.parts for i in range(n)], np.int32)
        )
    return rounds


def score_kernel(acts, basis, precond, weight, scores, sums):
    step, seqs = pl.program_id(0), acts.shape[0] // SEQ_TOK
    rows_in = jnp.dot(acts[...], basis[...], preferred_element_type=jnp.float32).astype(jnp.bfloat16)
    mixed = lax.dot_general(
        rows_in, precond[...], (((1,), (1,)), ((), ())), preferred_element_type=jnp.float32
    )
    mixed = mixed * jnp.concatenate([weight[...].astype(jnp.float32)] * VOTES, axis=1)
    for i in range(seqs):
        part = mixed[i * SEQ_TOK : (i + 1) * SEQ_TOK]
        sums[pl.ds(step * seqs + i, 1), :] = jnp.sum(part, axis=0, keepdims=True)

    @pl.when(step == pl.num_programs(0) - 1)
    def _():
        width = weight.shape[1]
        total = sums[...]
        scores[...] = jnp.concatenate(
            [jnp.sum(total[:, v * width : (v + 1) * width], axis=1, keepdims=True) for v in range(VOTES)],
            axis=1,
        )


def score_rows(acts, basis, precond, weight):
    tokens, width_in = acts.shape
    rows = 2 * SEQ_TOK
    whole = lambda a: pl.BlockSpec(a.shape, lambda i: (0, 0), pipeline_mode=pl.Buffered(1))
    return pl.pallas_call(
        score_kernel,
        grid=(tokens // rows,),
        in_specs=[
            pl.BlockSpec((rows, width_in), lambda i: (i, 0)),
            whole(basis),
            whole(precond),
            pl.BlockSpec((rows, weight.shape[1]), lambda i: (i, 0)),
        ],
        out_specs=pl.BlockSpec((tokens // SEQ_TOK, VOTES), lambda i: (0, 0)),
        out_shape=jax.ShapeDtypeStruct((tokens // SEQ_TOK, VOTES), jnp.float32),
        scratch_shapes=[pltpu.VMEM((tokens // SEQ_TOK, precond.shape[0]), jnp.float32)],
        compiler_params=pltpu.CompilerParams(vmem_limit_bytes=40 * 1024 * 1024),
        cost_estimate=pl.CostEstimate(
            flops=2 * tokens * basis.shape[1] * (width_in + precond.shape[0]),
            bytes_accessed=2 * (acts.size + basis.size + precond.size),
            transcendentals=0,
        ),
    )(acts, basis, precond, weight)


def shards(
    train_acts, train_grads, query_acts, query_grads, in_basis, out_basis, eig_values, vote_of_query
):
    core, x, y = lax.axis_index("core"), lax.axis_index("tensor"), lax.axis_index("y")
    train_local, query_local = train_acts.shape[1], query_acts.shape[1]
    local = train_local + query_local
    width_in, columns = in_basis.shape[1], in_basis.shape[2]
    depth = width_in // 2
    block, width_out = out_basis.shape[1], out_basis.shape[2]
    queries = vote_of_query.shape[0]
    eig_local = eig_values[0]

    def by_core(mine, other):
        return jnp.where(core == 0, mine, other), jnp.where(core == 0, other, mine)

    def halves(a, axis):
        mine = lax.dynamic_slice_in_dim(a, core * depth, depth, axis)
        other = lax.dynamic_slice_in_dim(a, (1 - core) * depth, depth, axis)
        return by_core(mine, shift(other, "core", 1))

    train_all = lax.all_gather(train_acts[0], ("y", "core", "tensor"), axis=0, tiled=True)
    query_block = jnp.concatenate(halves(query_acts[0], 1), axis=0)
    basis_mine = lax.dynamic_slice_in_dim(in_basis[0], core * depth, depth, 0)
    basis_other = lax.dynamic_slice_in_dim(in_basis[0], (1 - core) * depth, depth, 0)
    basis = jnp.concatenate([basis_mine, shift(basis_other, "core", 1)], axis=1)

    def grads_for(dx):
        at = lax.rem(x + dx, RING) * block
        return jnp.concatenate(
            [lax.dynamic_slice_in_dim(g[0], at, block, 1) for g in (train_grads, query_grads)], axis=0
        )

    grads = [grads_for(0)] + [shift(grads_for(dx), "tensor", dx) for dx in (1, 2, 3)]
    partial = [
        jnp.dot(grads[-e % RING], out_basis[0], preferred_element_type=jnp.float32) for e in range(RING)
    ]
    eig_row = jnp.full((8, width_out), jnp.sum(eig_local), jnp.float32)
    partial = jnp.concatenate(partial + [eig_row], axis=0)
    total = partial
    for k in (1, 2, 3):
        other = shift(partial, "tensor", k)
        total = total + jnp.concatenate(
            [other[((e + k) % RING) * local : ((e + k) % RING + 1) * local] for e in range(RING)]
            + [other[RING * local :]],
            axis=0,
        )
    eig_high = total[RING * local :].astype(jnp.bfloat16)
    eig_low = (total[RING * local :] - eig_high.astype(jnp.float32)).astype(jnp.bfloat16)
    out_x = jnp.concatenate([total[: RING * local].astype(jnp.bfloat16), eig_high, eig_low], axis=0)
    pair = jnp.stack(by_core(out_x, shift(out_x, "core", 1)))
    stack = jnp.stack([pair] + [shift(pair, "y", -dy) for dy in (1, 2, 3)])
    eig_sum = jnp.sum(stack[:, :, RING * local :, 0].astype(jnp.float32)) / 8.0
    damping = 0.1 * eig_sum / (eig_local.shape[0] * width_in)
    out_rows = stack[:, :, : RING * local].reshape(RING, 2, RING, local, width_out).swapaxes(1, 2)
    out_train = out_rows[:, :, :, :train_local].reshape(-1, width_out)
    out_query = out_rows[:, :, :, train_local:].reshape(-1, width_out)

    def in_order(a, rounds, rows):
        at = np.concatenate([(r[:, 1] * RING + r[:, 0]) * rows + r[:, 2] for r in rounds])
        pick = jnp.asarray(np.eye(a.shape[0], dtype=np.float32)[at], jnp.bfloat16)
        return jnp.dot(pick, a, preferred_element_type=jnp.float32).astype(jnp.bfloat16)

    def token_ids(rounds, rows):
        all_rows = np.concatenate(rounds)
        per = rows // 2
        sx = lax.rem(x + all_rows[:, 0], RING)
        sy = lax.rem(y + all_rows[:, 1], RING)
        sc = all_rows[:, 2] // per
        return ((sy * 2 + sc) * RING + sx) * per + all_rows[:, 2] % per

    def multiply(messages):
        return jnp.dot(jnp.concatenate(messages, axis=0), basis, preferred_element_type=jnp.float32)

    q_rows, q_half = 2 * query_local, query_local
    q1 = spread_1(query_block)
    q2 = spread_2(q1, q_rows, q_half)
    q3 = spread_3(q2, q_rows, q_half)
    q4 = spread_4(q3, q_rows, q_half)

    q_order = order_of(q_rows, q_half)
    q_in = jnp.concatenate([multiply([query_block] + q1), multiply(q2), multiply(q3 + q4)], axis=0)
    query_in = (q_in[:, :columns] + shift(q_in[:, columns:], "core", 1)).astype(jnp.bfloat16)
    query_id = token_ids(q_order, q_rows) // QT
    votes = jnp.sum(
        jnp.where(query_id[:, None] == jnp.arange(queries)[None, :], vote_of_query[None, :], 0), axis=1
    )
    by_vote = (votes[:, None] == jnp.arange(VOTES)[None, :]).astype(jnp.bfloat16)
    query_out = in_order(out_query, q_order, q_rows)
    spread_out = (by_vote[:, :, None] * query_out[:, None, :]).reshape(-1, VOTES * width_out)
    query_rot = lax.dot_general(
        spread_out, query_in, (((0,), (0,)), ((), ())), preferred_element_type=jnp.float32
    )
    precond = query_rot.reshape(VOTES, width_out, columns) / (eig_local + damping)
    precond = precond.astype(jnp.bfloat16).reshape(VOTES * width_out, columns)

    every = np.array([(dx, dy, r) for dy in range(RING) for dx in range(RING) for r in range(2 * train_local)])
    tokens = every.shape[0]
    train_id = token_ids([every.astype(np.int32)], 2 * train_local)
    pick = (jnp.arange(tokens)[:, None] == train_id[None, :]).astype(jnp.bfloat16)
    train_out = jnp.dot(pick, out_train, preferred_element_type=jnp.float32).astype(jnp.bfloat16)
    score_scale = 1.0 / math.sqrt(width_out * width_in * lax.axis_size("layer") * queries)
    scores = score_rows(train_all, in_basis[0], precond, train_out).T * score_scale

    plane = ("y", "core", "tensor")
    copies = jnp.broadcast_to(scores[None], (lax.axis_size(plane),) + scores.shape)
    scores = jnp.sum(lax.all_to_all(copies, plane, 0, 0, tiled=True), axis=0)
    layers, step = lax.axis_size("layer"), 1
    while step < layers:
        scores = scores + lax.ppermute(scores, "layer", [(i, i ^ step) for i in range(layers)])
        step *= 2
    return scores


def solution(mesh):
    fine = Mesh(mesh.devices.reshape(RING, 2, -1, RING), ("y", "core", "layer", "tensor"))
    rows = ("y", "core", "tensor")
    placed = (
        P("layer", rows, None),
        P("layer", rows, None),
        P("layer", rows, None),
        P("layer", rows, None),
        P("layer", None, rows),
        P("layer", "tensor", None),
        P("layer", None, rows),
        P(),
    )
    return jax.shard_map(shards, mesh=fine, in_specs=placed, out_specs=P(), check_vma=False)
```

```python
import functools
import math

import jax
import jax.numpy as jnp
import numpy as np
from jax import lax
from jax.experimental import pallas as pl
from jax.experimental.pallas import tpu as pltpu
from jax.sharding import Mesh
from jax.sharding import PartitionSpec as P

QT = 8
SEQ_TOK = 128
VOTES = 8
RING = 4
RING_ORDER = (0, 3, 1, 2)
VMEM = 48 * 1024 * 1024


def shift(a, axis, step):
    n = lax.axis_size(axis)
    return lax.ppermute(a, axis, [(i, (i + step) % n) for i in range(n)])


def together(*arrays):
    return lax.optimization_barrier(arrays)


def bundle(own, axis):
    return jnp.concatenate([own, shift(own, axis, 1), shift(own, axis, -1), shift(own, axis, 2)], axis=0)


def neighbours(by_x, by_y):
    return shift(by_x, "y", 1), shift(by_x, "y", -1), shift(by_y, "tensor", 1), shift(by_y, "tensor", -1)


def split_kernel(*refs):
    for source, target in zip(refs[:4], refs[4:]):
        target[...] = source[...]


def halves(four):
    half, width = four[0].shape[0] // 2, four[0].shape[1]
    steps = 4
    return pl.pallas_call(
        split_kernel,
        grid=(steps,),
        in_specs=[pl.BlockSpec((half, width // steps), lambda j, at=i % 2: (at, j)) for i in range(4)],
        out_specs=[pl.BlockSpec((half, width // steps), lambda j: (0, j))] * 4,
        out_shape=[jax.ShapeDtypeStruct((half, width), four[0].dtype)] * 4,
        cost_estimate=pl.CostEstimate(flops=1, bytes_accessed=1, transcendentals=0),
    )(*four)


def opposite(parts):
    a, b, c, d = parts
    return shift(a, "y", 1), shift(b, "y", -1), shift(c, "tensor", 1), shift(d, "tensor", -1)


def sources(x, y):
    by_x = lambda those: [(dy, dx, 0) for dy in those for dx in RING_ORDER]
    by_y = lambda those: [(dy, dx, 1) for dx in those for dy in RING_ORDER]
    at = by_x((0,)) + by_y((0,)) + by_x((3, 1)) + by_y((3, 1)) + by_x((2,)) + by_y((2,))
    at = np.array(at, np.int32)
    return lax.rem(at[:, 0] + y, RING), lax.rem(at[:, 1] + x, RING), at[:, 2]


def rotate_step(acts, bases, sums):
    rows = jnp.concatenate([a[...] for a in acts], axis=0)
    for basis, total in zip(bases, sums):
        part = jnp.dot(rows, basis[...], preferred_element_type=jnp.float32)

        @pl.when(pl.program_id(0) == 0)
        def _():
            total[...] = part

        @pl.when(pl.program_id(0) > 0)
        def _():
            total[...] += part


def early_kernel(count, *refs):
    mine, other, out, sum_mine, sum_other = refs[count:]
    rotate_step(refs[:count], (mine, other), (sum_mine, sum_other))

    @pl.when(pl.program_id(0) == pl.num_programs(0) - 1)
    def _():
        out[...] = jnp.concatenate([sum_mine[...], sum_other[...]], axis=1).astype(jnp.bfloat16)


def late_kernel(count, *refs):
    mine, other, votes, rotated, rot_early, out, rot, sum_mine, sum_other = refs[count:]
    rotate_step(refs[:count], (mine, other), (sum_mine, sum_other))

    @pl.when(pl.program_id(0) == pl.num_programs(0) - 1)
    def _():
        late = jnp.concatenate([sum_mine[...], sum_other[...]], axis=1).astype(jnp.bfloat16)
        out[...] = late
        rows, width = rotated.shape
        asked = late[late.shape[0] - rows :]
        for v in range(VOTES):
            at = slice(v * width, (v + 1) * width)
            spread = jnp.where(votes[...] == v, rotated[...], jnp.zeros_like(rotated))
            rot[:, at] = rot_early[:, at] + lax.dot_general(
                asked, spread, (((0,), (0,)), ((), ())), preferred_element_type=jnp.float32
            )


def final_kernel(group, rot, rot_other, eig, early, late, weight, scores):
    width = weight.shape[1]
    columns = rot.shape[0] // 2
    rows_in = jnp.concatenate([early[...], late[...]], axis=0)
    for v in range(VOTES):
        at = slice(v * width, (v + 1) * width)
        total = rot[:, at] + jnp.concatenate([rot_other[columns:, at], rot_other[:columns, at]], axis=0)
        precond = (total / eig[...]).astype(jnp.bfloat16)
        mixed = jnp.dot(rows_in, precond, preferred_element_type=jnp.float32)
        mixed = (mixed * weight[...].astype(jnp.float32)).reshape(-1, group, width)
        scores[:, at] = jnp.sum(mixed, axis=1)


def call_rotate(kernel, acts, bases, extra, results):
    steps = 2
    depth, columns = bases[0].shape[0] // steps, bases[0].shape[1]
    total = sum(a.shape[0] for a in acts)
    return pl.pallas_call(
        kernel,
        grid=(steps,),
        in_specs=[pl.BlockSpec((a.shape[0], depth), lambda i: (0, i)) for a in acts]
        + [pl.BlockSpec((depth, columns), lambda i: (i, 0))] * 2
        + [pl.BlockSpec(a.shape, lambda i: (0, 0), pipeline_mode=pl.Buffered(1)) for a in extra],
        out_specs=[pl.BlockSpec(r.shape, lambda i: (0, 0)) for r in results],
        out_shape=results,
        scratch_shapes=[pltpu.VMEM((total, columns), jnp.float32)] * 2,
        compiler_params=pltpu.CompilerParams(vmem_limit_bytes=VMEM),
        cost_estimate=pl.CostEstimate(flops=1, bytes_accessed=1, transcendentals=0),
    )(*acts, *bases, *extra)


def rotate(acts, bases):
    total = sum(a.shape[0] for a in acts)
    result = jax.ShapeDtypeStruct((total, 2 * bases[0].shape[1]), jnp.bfloat16)
    return call_rotate(functools.partial(early_kernel, len(acts)), acts, bases, (), [result])[0]


def shards(
    train_acts, train_grads, query_acts, query_grads, in_basis, out_basis, eig_values, vote_of_query
):
    core, x, y = lax.axis_index("core"), lax.axis_index("tensor"), lax.axis_index("y")
    plane = ("y", "core", "tensor")
    devices = lax.axis_size(plane)
    train_local, query_local = train_acts.shape[1], query_acts.shape[1]
    local = train_local + query_local
    width_in, columns = in_basis.shape[1], in_basis.shape[2]
    block, width = out_basis.shape[1], out_basis.shape[2]
    queries = vote_of_query.shape[0]
    mine = in_basis[0]

    part = local // 2
    b1 = bundle(train_acts[0, :part], "tensor"), bundle(
        jnp.concatenate([train_acts[0, part:], query_acts[0]], axis=0), "y"
    )
    grads = jnp.concatenate(
        [g[0, :, j * block : (j + 1) * block] for j in range(RING) for g in (train_grads, query_grads)], axis=0
    )
    grads = lax.all_to_all(grads, "tensor", 0, 0, tiled=True)
    by_y, grads = together(b1[1], grads)
    b1 = (b1[0], by_y)
    b2 = neighbours(*b1)
    bases = (mine, shift(mine, "core", 1))
    first = rotate(list(b1), bases)

    partial = jnp.dot(grads, out_basis[0], preferred_element_type=jnp.float32)
    partial = lax.all_to_all(partial, "tensor", 0, 0, tiled=True)
    partial, first = together(partial, first)
    b2, first = together(b2, first)
    parts = halves(b2)
    b3 = opposite(parts)
    out_local = jnp.sum(partial.reshape(RING, local, width), axis=0).astype(jnp.bfloat16)
    eig_part = jnp.full((8, width), jnp.sum(eig_values), jnp.float32)
    eig_high = eig_part.astype(jnp.bfloat16)
    eig_low = (eig_part - eig_high.astype(jnp.float32)).astype(jnp.bfloat16)
    out_local = jnp.concatenate([out_local, eig_high, eig_low], axis=0)
    copies = jnp.broadcast_to(out_local[None], (devices,) + out_local.shape)
    out_all = lax.all_to_all(copies, plane, 0, 0, tiled=True)
    out_all, *b2 = together(out_all, *b2)
    eig_sum = jnp.sum(out_all[:, local:, 0].astype(jnp.float32)) / 8.0
    damping = 0.1 * eig_sum / (eig_values.shape[1] * width_in)
    eig = eig_values[0].T
    eig = jnp.concatenate([eig, shift(eig, "core", 1)], axis=0) + damping

    group_y, group_x, half = sources(x, y)
    device = (group_y * 2 + core) * RING + group_x
    inside = half[:, None] * part + np.arange(part)[None, :]
    asked = inside.reshape(-1) >= train_local
    ids = (device[:, None] * local + inside).reshape(-1)
    query = (device[:, None] * query_local + inside - train_local) // QT
    out_rows = out_all[:, :local].reshape(-1, width)
    pick = (ids[:, None] == jnp.arange(out_rows.shape[0])[None, :]).astype(jnp.bfloat16)
    rotated = jnp.dot(pick, out_rows, preferred_element_type=jnp.float32).astype(jnp.bfloat16)
    weight = jnp.where(asked[:, None], jnp.zeros_like(rotated), rotated)
    votes = jnp.sum(
        jnp.where(query.reshape(-1)[:, None] == jnp.arange(queries)[None, :], vote_of_query[None, :], 0), axis=1
    )
    votes = jnp.where(asked, votes, -1)

    second = rotate(list(b2), bases)
    early = jnp.concatenate([first, second], axis=0)
    early_rows = early.shape[0]
    late_rows = sum(a.shape[0] for a in b3)
    kind = lambda rows: jax.ShapeDtypeStruct((rows, 2 * columns), jnp.bfloat16)
    t, n = first.shape[0] // 2, second.shape[0] // 2
    ask = lambda a: jnp.concatenate([a[t : 2 * t], a[2 * t + n : 2 * t + 2 * n]], axis=0)
    by_vote = (ask(votes)[:, None] == jnp.arange(VOTES)[None, :]).astype(jnp.bfloat16)
    spread = (by_vote[:, :, None] * ask(rotated)[:, None, :]).reshape(-1, VOTES * width)
    rot_early = lax.dot_general(
        jnp.concatenate([first[t:], second[n:]], axis=0),
        spread,
        (((0,), (0,)), ((), ())),
        preferred_element_type=jnp.float32,
    )
    tail = slice(early_rows + late_rows // 2, early_rows + late_rows)
    late, rot = call_rotate(
        functools.partial(late_kernel, len(b3)),
        b3,
        bases,
        (votes[tail, None], rotated[tail], rot_early),
        [kind(late_rows), jax.ShapeDtypeStruct(rot_early.shape, jnp.float32)],
    )
    sums = (rot, shift(rot, "core", 1), eig, early, late, weight)
    by_group = pl.pallas_call(
        functools.partial(final_kernel, part),
        out_shape=jax.ShapeDtypeStruct((device.shape[0], VOTES * width), jnp.float32),
        in_specs=[pl.BlockSpec(memory_space=pltpu.VMEM)] * len(sums),
        out_specs=pl.BlockSpec(memory_space=pltpu.VMEM),
        compiler_params=pltpu.CompilerParams(vmem_limit_bytes=VMEM),
    )(*sums)
    by_group = jnp.sum(by_group.reshape(-1, VOTES, width), axis=2)
    seq = (group_y * 2 + core) * (RING * train_local) // SEQ_TOK
    seqs = devices * train_local // SEQ_TOK
    score_scale = 1.0 / math.sqrt(width * width_in * lax.axis_size("layer") * queries)
    of_seq = seq[:, None, None] == jnp.arange(seqs)[None, None, :]
    scores = jnp.sum(jnp.where(of_seq, by_group[:, :, None], 0.0), axis=0) * score_scale

    copies = jnp.broadcast_to(scores[None], (devices,) + scores.shape)
    scores = jnp.sum(lax.all_to_all(copies, plane, 0, 0, tiled=True), axis=0)
    layers, step = lax.axis_size("layer"), 1
    while step < layers:
        scores = scores + lax.ppermute(scores, "layer", [(i, i ^ step) for i in range(layers)])
        step *= 2
    return scores


def solution(mesh):
    fine = Mesh(mesh.devices.reshape(RING, 2, -1, RING), ("y", "core", "layer", "tensor"))
    rows = ("y", "core", "tensor")
    placed = (
        P("layer", rows, None),
        P("layer", rows, None),
        P("layer", rows, None),
        P("layer", rows, None),
        P("layer", None, rows),
        P("layer", "tensor", None),
        P("layer", None, rows),
        P(),
    )
    return jax.shard_map(shards, mesh=fine, in_specs=placed, out_specs=P(), check_vma=False)
```

```python
import functools
import math

import jax
import jax.numpy as jnp
import numpy as np
from jax import lax
from jax.experimental import pallas as pl
from jax.experimental.pallas import tpu as pltpu
from jax.sharding import Mesh
from jax.sharding import PartitionSpec as P

QT = 8
SEQ_TOK = 128
VOTES = 8
RING = 4
RING_ORDER = (0, 3, 1, 2)
VMEM = 48 * 1024 * 1024


def shift(a, axis, step):
    n = lax.axis_size(axis)
    return lax.ppermute(a, axis, [(i, (i + step) % n) for i in range(n)])


def together(*arrays):
    return lax.optimization_barrier(arrays)


def bundle(own, axis):
    return jnp.concatenate([own, shift(own, axis, 1), shift(own, axis, -1), shift(own, axis, 2)], axis=0)


def neighbours(by_x, by_y):
    return shift(by_x, "y", 1), shift(by_x, "y", -1), shift(by_y, "tensor", 1), shift(by_y, "tensor", -1)


def split_kernel(*refs):
    for source, target in zip(refs[:4], refs[4:]):
        target[...] = source[...]


def halves(four):
    half, width = four[0].shape[0] // 2, four[0].shape[1]
    steps = 2
    return pl.pallas_call(
        split_kernel,
        grid=(steps,),
        in_specs=[pl.BlockSpec((half, width // steps), lambda j, at=i % 2: (at, j)) for i in range(4)],
        out_specs=[pl.BlockSpec((half, width // steps), lambda j: (0, j))] * 4,
        out_shape=[jax.ShapeDtypeStruct((half, width), four[0].dtype)] * 4,
        compiler_params=pltpu.CompilerParams(vmem_limit_bytes=16 * 1024 * 1024),
        cost_estimate=pl.CostEstimate(flops=1, bytes_accessed=1, transcendentals=0),
    )(*four)


def opposite(parts):
    a, b, c, d = parts
    return shift(a, "y", 1), shift(b, "y", -1), shift(c, "tensor", 1), shift(d, "tensor", -1)


def sources(x, y):
    by_x = lambda those: [(dy, dx, 0) for dy in those for dx in RING_ORDER]
    by_y = lambda those: [(dy, dx, 1) for dx in those for dy in RING_ORDER]
    at = by_x((0,)) + by_y((0,)) + by_x((3, 1)) + by_y((3, 1)) + by_x((2,)) + by_y((2,))
    at = np.array(at, np.int32)
    return lax.rem(at[:, 0] + y, RING), lax.rem(at[:, 1] + x, RING), at[:, 2]


def rotate_step(acts, bases, sums):
    rows = jnp.concatenate([a[...] for a in acts], axis=0)
    for basis, total in zip(bases, sums):
        part = jnp.dot(rows, basis[...], preferred_element_type=jnp.float32)

        @pl.when(pl.program_id(0) == 0)
        def _():
            total[...] = part

        @pl.when(pl.program_id(0) > 0)
        def _():
            total[...] += part


def early_kernel(count, *refs):
    mine, other, out, sum_mine, sum_other = refs[count:]
    rotate_step(refs[:count], (mine, other), (sum_mine, sum_other))

    @pl.when(pl.program_id(0) == pl.num_programs(0) - 1)
    def _():
        out[...] = jnp.concatenate([sum_mine[...], sum_other[...]], axis=1).astype(jnp.bfloat16)


def late_kernel(count, *refs):
    mine, other, votes, rotated, rot_early, out, rot, sum_mine, sum_other = refs[count:]
    rotate_step(refs[:count], (mine, other), (sum_mine, sum_other))

    @pl.when(pl.program_id(0) == pl.num_programs(0) - 1)
    def _():
        late = jnp.concatenate([sum_mine[...], sum_other[...]], axis=1).astype(jnp.bfloat16)
        out[...] = late
        rows, width = rotated.shape
        asked = late[late.shape[0] - rows :]
        spread = jnp.concatenate(
            [jnp.where(votes[...] == v, rotated[...], jnp.zeros_like(rotated)) for v in range(VOTES)], axis=1
        )
        rot[...] = rot_early[...] + lax.dot_general(
            asked, spread, (((0,), (0,)), ((), ())), preferred_element_type=jnp.float32
        )


def final_kernel(group, rot, rot_other, eig, early, late, weight, scores):
    width = weight.shape[1]
    columns = rot.shape[0] // 2
    rows_in = jnp.concatenate([early[...], late[...]], axis=0)
    factor = weight[...].astype(jnp.float32)
    for v in range(0, VOTES, 2):
        at = slice(v * width, (v + 2) * width)
        total = rot[:, at] + jnp.concatenate([rot_other[columns:, at], rot_other[:columns, at]], axis=0)
        precond = (total / jnp.concatenate([eig[...]] * 2, axis=1)).astype(jnp.bfloat16)
        mixed = jnp.dot(rows_in, precond, preferred_element_type=jnp.float32)
        mixed = (mixed * jnp.concatenate([factor] * 2, axis=1)).reshape(-1, group, 2 * width)
        scores[:, at] = jnp.sum(mixed, axis=1)


def call_rotate(kernel, acts, bases, extra, results):
    steps = 2
    depth, columns = bases[0].shape[0] // steps, bases[0].shape[1]
    total = sum(a.shape[0] for a in acts)
    return pl.pallas_call(
        kernel,
        grid=(steps,),
        in_specs=[pl.BlockSpec((a.shape[0], depth), lambda i: (0, i)) for a in acts]
        + [pl.BlockSpec((depth, columns), lambda i: (i, 0))] * 2
        + [pl.BlockSpec(a.shape, lambda i: (0, 0), pipeline_mode=pl.Buffered(1)) for a in extra],
        out_specs=[pl.BlockSpec(r.shape, lambda i: (0, 0)) for r in results],
        out_shape=results,
        scratch_shapes=[pltpu.VMEM((total, columns), jnp.float32)] * 2,
        compiler_params=pltpu.CompilerParams(vmem_limit_bytes=VMEM),
        cost_estimate=pl.CostEstimate(flops=1, bytes_accessed=1, transcendentals=0),
    )(*acts, *bases, *extra)


def rotate(acts, bases):
    total = sum(a.shape[0] for a in acts)
    result = jax.ShapeDtypeStruct((total, 2 * bases[0].shape[1]), jnp.bfloat16)
    return call_rotate(functools.partial(early_kernel, len(acts)), acts, bases, (), [result])[0]


def shards(
    train_acts, train_grads, query_acts, query_grads, in_basis, out_basis, eig_values, vote_of_query
):
    core, x, y = lax.axis_index("core"), lax.axis_index("tensor"), lax.axis_index("y")
    plane = ("y", "core", "tensor")
    devices = lax.axis_size(plane)
    train_local, query_local = train_acts.shape[1], query_acts.shape[1]
    local = train_local + query_local
    width_in, columns = in_basis.shape[1], in_basis.shape[2]
    block, width = out_basis.shape[1], out_basis.shape[2]
    queries = vote_of_query.shape[0]
    mine = in_basis[0]

    part = local // 2
    b1 = bundle(train_acts[0, :part], "tensor"), bundle(
        jnp.concatenate([train_acts[0, part:], query_acts[0]], axis=0), "y"
    )
    grads = jnp.concatenate(
        [g[0, :, j * block : (j + 1) * block] for j in range(RING) for g in (train_grads, query_grads)], axis=0
    )
    grads = lax.all_to_all(grads, "tensor", 0, 0, tiled=True)
    by_y, grads = together(b1[1], grads)
    b1 = (b1[0], by_y)
    b2 = neighbours(*b1)
    bases = (mine, shift(mine, "core", 1))
    first = rotate(list(b1), bases)

    partial = jnp.dot(grads, out_basis[0], preferred_element_type=jnp.float32)
    partial = lax.all_to_all(partial, "tensor", 0, 0, tiled=True)
    partial, first = together(partial, first)
    b2, first = together(b2, first)
    parts = halves(b2)
    b3 = opposite(parts)
    out_local = jnp.sum(partial.reshape(RING, local, width), axis=0).astype(jnp.bfloat16)
    eig_part = jnp.full((8, width), jnp.sum(eig_values), jnp.float32)
    eig_high = eig_part.astype(jnp.bfloat16)
    eig_low = (eig_part - eig_high.astype(jnp.float32)).astype(jnp.bfloat16)
    out_local = jnp.concatenate([out_local, eig_high, eig_low], axis=0)
    copies = jnp.broadcast_to(out_local[None], (devices,) + out_local.shape)
    out_all = lax.all_to_all(copies, plane, 0, 0, tiled=True)
    out_all, *b2 = together(out_all, *b2)
    eig_sum = jnp.sum(out_all[:, local:, 0].astype(jnp.float32)) / 8.0
    damping = 0.1 * eig_sum / (eig_values.shape[1] * width_in)
    eig = eig_values[0].T
    eig = jnp.concatenate([eig, shift(eig, "core", 1)], axis=0) + damping

    group_y, group_x, half = sources(x, y)
    device = (group_y * 2 + core) * RING + group_x
    inside = half[:, None] * part + np.arange(part)[None, :]
    asked = inside.reshape(-1) >= train_local
    ids = (device[:, None] * local + inside).reshape(-1)
    query = (device[:, None] * query_local + inside - train_local) // QT
    out_rows = out_all[:, :local].reshape(-1, width)
    pick = (ids[:, None] == jnp.arange(out_rows.shape[0])[None, :]).astype(jnp.bfloat16)
    rotated = jnp.dot(pick, out_rows, preferred_element_type=jnp.float32).astype(jnp.bfloat16)
    weight = jnp.where(asked[:, None], jnp.zeros_like(rotated), rotated)
    votes = jnp.sum(
        jnp.where(query.reshape(-1)[:, None] == jnp.arange(queries)[None, :], vote_of_query[None, :], 0), axis=1
    )
    votes = jnp.where(asked, votes, -1)

    second = rotate(list(b2), bases)
    early = jnp.concatenate([first, second], axis=0)
    early_rows = early.shape[0]
    late_rows = sum(a.shape[0] for a in b3)
    kind = lambda rows: jax.ShapeDtypeStruct((rows, 2 * columns), jnp.bfloat16)
    t, n = first.shape[0] // 2, second.shape[0] // 2
    ask = lambda a: jnp.concatenate([a[t : 2 * t], a[2 * t + n : 2 * t + 2 * n]], axis=0)
    by_vote = (ask(votes)[:, None] == jnp.arange(VOTES)[None, :]).astype(jnp.bfloat16)
    spread = (by_vote[:, :, None] * ask(rotated)[:, None, :]).reshape(-1, VOTES * width)
    rot_early = lax.dot_general(
        jnp.concatenate([first[t:], second[n:]], axis=0),
        spread,
        (((0,), (0,)), ((), ())),
        preferred_element_type=jnp.float32,
    )
    tail = slice(early_rows + late_rows // 2, early_rows + late_rows)
    late, rot = call_rotate(
        functools.partial(late_kernel, len(b3)),
        b3,
        bases,
        (votes[tail, None], rotated[tail], rot_early),
        [kind(late_rows), jax.ShapeDtypeStruct(rot_early.shape, jnp.float32)],
    )
    sums = (rot, shift(rot, "core", 1), eig, early, late, weight)
    by_group = pl.pallas_call(
        functools.partial(final_kernel, part),
        out_shape=jax.ShapeDtypeStruct((device.shape[0], VOTES * width), jnp.float32),
        in_specs=[pl.BlockSpec(memory_space=pltpu.VMEM)] * len(sums),
        out_specs=pl.BlockSpec(memory_space=pltpu.VMEM),
        compiler_params=pltpu.CompilerParams(vmem_limit_bytes=VMEM),
    )(*sums)
    by_group = jnp.sum(by_group.reshape(-1, VOTES, width), axis=2)
    seq = (group_y * 2 + core) * (RING * train_local) // SEQ_TOK
    seqs = devices * train_local // SEQ_TOK
    score_scale = 1.0 / math.sqrt(width * width_in * lax.axis_size("layer") * queries)
    of_seq = seq[:, None, None] == jnp.arange(seqs)[None, None, :]
    scores = jnp.sum(jnp.where(of_seq, by_group[:, :, None], 0.0), axis=0) * score_scale

    copies = jnp.broadcast_to(scores[None], (devices,) + scores.shape)
    scores = jnp.sum(lax.all_to_all(copies, plane, 0, 0, tiled=True), axis=0)
    layers, step = lax.axis_size("layer"), 1
    while step < layers:
        scores = scores + lax.ppermute(scores, "layer", [(i, i ^ step) for i in range(layers)])
        step *= 2
    return scores


def solution(mesh):
    fine = Mesh(mesh.devices.reshape(RING, 2, -1, RING), ("y", "core", "layer", "tensor"))
    rows = ("y", "core", "tensor")
    placed = (
        P("layer", rows, None),
        P("layer", rows, None),
        P("layer", rows, None),
        P("layer", rows, None),
        P("layer", None, rows),
        P("layer", "tensor", None),
        P("layer", None, rows),
        P(),
    )
    return jax.shard_map(shards, mesh=fine, in_specs=placed, out_specs=P(), check_vma=False)
```

```python
import functools
import math

import jax
import jax.numpy as jnp
import numpy as np
from jax import lax
from jax.experimental import pallas as pl
from jax.experimental.pallas import tpu as pltpu
from jax.sharding import Mesh
from jax.sharding import PartitionSpec as P

QT = 8
SEQ_TOK = 128
VOTES = 8
RING = 4
RING_ORDER = (0, 3, 1, 2)
VMEM = 48 * 1024 * 1024


def shift(a, axis, step):
    n = lax.axis_size(axis)
    return lax.ppermute(a, axis, [(i, (i + step) % n) for i in range(n)])


def together(*arrays):
    return lax.optimization_barrier(arrays)


def bundle(own, axis):
    return jnp.concatenate([own, shift(own, axis, 1), shift(own, axis, -1), shift(own, axis, 2)], axis=0)


def neighbours(by_x, by_y):
    return shift(by_x, "y", 1), shift(by_x, "y", -1), shift(by_y, "tensor", 1), shift(by_y, "tensor", -1)


def split_kernel(*refs):
    for source, target in zip(refs[:4], refs[4:]):
        target[...] = source[...]


def halves(four):
    half, width = four[0].shape[0] // 2, four[0].shape[1]
    steps = 1
    return pl.pallas_call(
        split_kernel,
        grid=(steps,),
        in_specs=[pl.BlockSpec((half, width // steps), lambda j, at=i % 2: (at, j)) for i in range(4)],
        out_specs=[pl.BlockSpec((half, width // steps), lambda j: (0, j))] * 4,
        out_shape=[jax.ShapeDtypeStruct((half, width), four[0].dtype)] * 4,
        compiler_params=pltpu.CompilerParams(vmem_limit_bytes=24 * 1024 * 1024),
        cost_estimate=pl.CostEstimate(flops=1, bytes_accessed=1, transcendentals=0),
    )(*four)


def opposite(parts):
    a, b, c, d = parts
    return shift(a, "y", 1), shift(b, "y", -1), shift(c, "tensor", 1), shift(d, "tensor", -1)


def sources(x, y):
    by_x = lambda those: [(dy, dx, 0) for dy in those for dx in RING_ORDER]
    by_y = lambda those: [(dy, dx, 1) for dx in those for dy in RING_ORDER]
    at = by_x((0,)) + by_y((0,)) + by_x((3, 1)) + by_y((3, 1)) + by_x((2,)) + by_y((2,))
    at = np.array(at, np.int32)
    return lax.rem(at[:, 0] + y, RING), lax.rem(at[:, 1] + x, RING), at[:, 2]


def rotate_step(acts, bases, sums):
    rows = jnp.concatenate([a[...] for a in acts], axis=0)
    for basis, total in zip(bases, sums):
        part = jnp.dot(rows, basis[...], preferred_element_type=jnp.float32)

        @pl.when(pl.program_id(0) == 0)
        def _():
            total[...] = part

        @pl.when(pl.program_id(0) > 0)
        def _():
            total[...] += part


def early_kernel(count, *refs):
    mine, other, out, sum_mine, sum_other = refs[count:]
    rotate_step(refs[:count], (mine, other), (sum_mine, sum_other))

    @pl.when(pl.program_id(0) == pl.num_programs(0) - 1)
    def _():
        out[...] = jnp.concatenate([sum_mine[...], sum_other[...]], axis=1).astype(jnp.bfloat16)


def late_kernel(count, *refs):
    mine, other, votes, rotated, rot_early, out, rot, sum_mine, sum_other = refs[count:]
    rotate_step(refs[:count], (mine, other), (sum_mine, sum_other))

    @pl.when(pl.program_id(0) == pl.num_programs(0) - 1)
    def _():
        late = jnp.concatenate([sum_mine[...], sum_other[...]], axis=1).astype(jnp.bfloat16)
        out[...] = late
        rows, width = rotated.shape
        asked = late[late.shape[0] - rows :]
        spread = jnp.concatenate(
            [jnp.where(votes[...] == v, rotated[...], jnp.zeros_like(rotated)) for v in range(VOTES)], axis=1
        )
        rot[...] = rot_early[...] + lax.dot_general(
            asked, spread, (((0,), (0,)), ((), ())), preferred_element_type=jnp.float32
        )


def final_kernel(group, rot, rot_other, eig, early, late, weight, scores):
    width = weight.shape[1]
    columns = rot.shape[0] // 2
    rows_in = jnp.concatenate([early[...], late[...]], axis=0)
    factor = weight[...].astype(jnp.float32)
    for v in range(0, VOTES, 2):
        at = slice(v * width, (v + 2) * width)
        total = rot[:, at] + jnp.concatenate([rot_other[columns:, at], rot_other[:columns, at]], axis=0)
        precond = (total / jnp.concatenate([eig[...]] * 2, axis=1)).astype(jnp.bfloat16)
        mixed = jnp.dot(rows_in, precond, preferred_element_type=jnp.float32)
        mixed = (mixed * jnp.concatenate([factor] * 2, axis=1)).reshape(-1, group, 2 * width)
        scores[:, at] = jnp.sum(mixed, axis=1)


def call_rotate(kernel, acts, bases, extra, results):
    steps = 2
    depth, columns = bases[0].shape[0] // steps, bases[0].shape[1]
    total = sum(a.shape[0] for a in acts)
    return pl.pallas_call(
        kernel,
        grid=(steps,),
        in_specs=[pl.BlockSpec((a.shape[0], depth), lambda i: (0, i)) for a in acts]
        + [pl.BlockSpec((depth, columns), lambda i: (i, 0))] * 2
        + [pl.BlockSpec(a.shape, lambda i: (0, 0), pipeline_mode=pl.Buffered(1)) for a in extra],
        out_specs=[pl.BlockSpec(r.shape, lambda i: (0, 0)) for r in results],
        out_shape=results,
        scratch_shapes=[pltpu.VMEM((total, columns), jnp.float32)] * 2,
        compiler_params=pltpu.CompilerParams(vmem_limit_bytes=VMEM),
        cost_estimate=pl.CostEstimate(flops=1, bytes_accessed=1, transcendentals=0),
    )(*acts, *bases, *extra)


def rotate(acts, bases):
    total = sum(a.shape[0] for a in acts)
    result = jax.ShapeDtypeStruct((total, 2 * bases[0].shape[1]), jnp.bfloat16)
    return call_rotate(functools.partial(early_kernel, len(acts)), acts, bases, (), [result])[0]


def shards(
    train_acts, train_grads, query_acts, query_grads, in_basis, out_basis, eig_values, vote_of_query
):
    core, x, y = lax.axis_index("core"), lax.axis_index("tensor"), lax.axis_index("y")
    plane = ("y", "core", "tensor")
    devices = lax.axis_size(plane)
    train_local, query_local = train_acts.shape[1], query_acts.shape[1]
    local = train_local + query_local
    width_in, columns = in_basis.shape[1], in_basis.shape[2]
    block, width = out_basis.shape[1], out_basis.shape[2]
    queries = vote_of_query.shape[0]
    mine = in_basis[0]

    part = local // 2
    b1 = bundle(train_acts[0, :part], "tensor"), bundle(
        jnp.concatenate([train_acts[0, part:], query_acts[0]], axis=0), "y"
    )
    grads = jnp.concatenate(
        [g[0, :, j * block : (j + 1) * block] for j in range(RING) for g in (train_grads, query_grads)], axis=0
    )
    grads = lax.all_to_all(grads, "tensor", 0, 0, tiled=True)
    by_y, grads = together(b1[1], grads)
    b1 = (b1[0], by_y)
    b2 = neighbours(*b1)
    bases = (mine, shift(mine, "core", 1))
    first = rotate(list(b1), bases)

    partial = jnp.dot(grads, out_basis[0], preferred_element_type=jnp.float32)
    partial = lax.all_to_all(partial, "tensor", 0, 0, tiled=True)
    partial, first = together(partial, first)
    b2, first = together(b2, first)
    parts = halves(b2)
    b3 = opposite(parts)
    out_local = jnp.sum(partial.reshape(RING, local, width), axis=0).astype(jnp.bfloat16)
    eig_part = jnp.full((8, width), jnp.sum(eig_values), jnp.float32)
    eig_high = eig_part.astype(jnp.bfloat16)
    eig_low = (eig_part - eig_high.astype(jnp.float32)).astype(jnp.bfloat16)
    out_local = jnp.concatenate([out_local, eig_high, eig_low], axis=0)
    copies = jnp.broadcast_to(out_local[None], (devices,) + out_local.shape)
    out_all = lax.all_to_all(copies, plane, 0, 0, tiled=True)
    out_all, *b2 = together(out_all, *b2)
    eig_sum = jnp.sum(out_all[:, local:, 0].astype(jnp.float32)) / 8.0
    damping = 0.1 * eig_sum / (eig_values.shape[1] * width_in)
    eig = eig_values[0].T
    eig = jnp.concatenate([eig, shift(eig, "core", 1)], axis=0) + damping

    group_y, group_x, half = sources(x, y)
    device = (group_y * 2 + core) * RING + group_x
    inside = half[:, None] * part + np.arange(part)[None, :]
    asked = inside.reshape(-1) >= train_local
    ids = (device[:, None] * local + inside).reshape(-1)
    query = (device[:, None] * query_local + inside - train_local) // QT
    out_rows = out_all[:, :local].reshape(-1, width)
    pick = (ids[:, None] == jnp.arange(out_rows.shape[0])[None, :]).astype(jnp.bfloat16)
    rotated = jnp.dot(pick, out_rows, preferred_element_type=jnp.float32).astype(jnp.bfloat16)
    weight = jnp.where(asked[:, None], jnp.zeros_like(rotated), rotated)
    votes = jnp.sum(
        jnp.where(query.reshape(-1)[:, None] == jnp.arange(queries)[None, :], vote_of_query[None, :], 0), axis=1
    )
    votes = jnp.where(asked, votes, -1)

    second = rotate(list(b2), bases)
    early = jnp.concatenate([first, second], axis=0)
    early_rows = early.shape[0]
    late_rows = sum(a.shape[0] for a in b3)
    kind = lambda rows: jax.ShapeDtypeStruct((rows, 2 * columns), jnp.bfloat16)
    t, n = first.shape[0] // 2, second.shape[0] // 2
    ask = lambda a: jnp.concatenate([a[t : 2 * t], a[2 * t + n : 2 * t + 2 * n]], axis=0)
    by_vote = (ask(votes)[:, None] == jnp.arange(VOTES)[None, :]).astype(jnp.bfloat16)
    spread = (by_vote[:, :, None] * ask(rotated)[:, None, :]).reshape(-1, VOTES * width)
    rot_early = lax.dot_general(
        jnp.concatenate([first[t:], second[n:]], axis=0),
        spread,
        (((0,), (0,)), ((), ())),
        preferred_element_type=jnp.float32,
    )
    tail = slice(early_rows + late_rows // 2, early_rows + late_rows)
    late, rot = call_rotate(
        functools.partial(late_kernel, len(b3)),
        b3,
        bases,
        (votes[tail, None], rotated[tail], rot_early),
        [kind(late_rows), jax.ShapeDtypeStruct(rot_early.shape, jnp.float32)],
    )
    sums = (rot, shift(rot, "core", 1), eig, early, late, weight)
    by_group = pl.pallas_call(
        functools.partial(final_kernel, part),
        out_shape=jax.ShapeDtypeStruct((device.shape[0], VOTES * width), jnp.float32),
        in_specs=[pl.BlockSpec(memory_space=pltpu.VMEM)] * len(sums),
        out_specs=pl.BlockSpec(memory_space=pltpu.VMEM),
        compiler_params=pltpu.CompilerParams(vmem_limit_bytes=VMEM),
    )(*sums)
    by_group = jnp.sum(by_group.reshape(-1, VOTES, width), axis=2)
    seq = (group_y * 2 + core) * (RING * train_local) // SEQ_TOK
    seqs = devices * train_local // SEQ_TOK
    score_scale = 1.0 / math.sqrt(width * width_in * lax.axis_size("layer") * queries)
    of_seq = seq[:, None, None] == jnp.arange(seqs)[None, None, :]
    scores = jnp.sum(jnp.where(of_seq, by_group[:, :, None], 0.0), axis=0) * score_scale

    copies = jnp.broadcast_to(scores[None], (devices,) + scores.shape)
    scores = jnp.sum(lax.all_to_all(copies, plane, 0, 0, tiled=True), axis=0)
    layers, step = lax.axis_size("layer"), 1
    while step < layers:
        scores = scores + lax.ppermute(scores, "layer", [(i, i ^ step) for i in range(layers)])
        step *= 2
    return scores


def solution(mesh):
    fine = Mesh(mesh.devices.reshape(RING, 2, -1, RING), ("y", "core", "layer", "tensor"))
    rows = ("y", "core", "tensor")
    placed = (
        P("layer", rows, None),
        P("layer", rows, None),
        P("layer", rows, None),
        P("layer", rows, None),
        P("layer", None, rows),
        P("layer", "tensor", None),
        P("layer", None, rows),
        P(),
    )
    return jax.shard_map(shards, mesh=fine, in_specs=placed, out_specs=P(), check_vma=False)
```
